512 devices in a mesh: replica: 32 (over z, y_lo, core), fsdp: 16 (over x, y_hi).
Axes of the slice: x: 4, y: 8 (y_hi: 4, y_lo: 2; y = y_hi * 2 + y_lo), z: 8, core: 2. Of those that a mesh axis runs over, the one named last changes fastest.
Arguments:
- features: bfloat16 [65536, 8192], P(('replica', 'fsdp')), may hold values from -6 to 6
- cotangents: bfloat16 [65536, 512], P(('replica', 'fsdp')), may hold values from -0.13183594 to 0.13183594
- params: bfloat16 [32, 512, 8192], P('replica', None, 'fsdp'), may hold values from -6.5 to 6.5
- first_moment: bfloat16 [32, 512, 8192], P('replica', None, 'fsdp'), may hold values from -5 to 5
- second_moment: bfloat16 [32, 512, 8192], P('replica', None, 'fsdp'), may hold values from 0.25 to 4
- anchor: float32 [512, 8192], P('replica', 'fsdp'), may hold values from -5 to 5
- outer_momentum: float32 [512, 8192], P('replica', 'fsdp'), may hold values from -0.5 to 0.5
- step: int32 [1], replicated, may hold values from 1 to 16
Outputs:
- merged: float32 [32, 512, 8192], P('replica', None, 'fsdp')
- momentum_next: float32 [512, 8192], P('replica', 'fsdp')
The draws below stay inside these ranges and needn't reach their ends.
All inputs are finite; a program needn't handle non-finite values.
Results may differ from the reference program's by a relative error of at most 0.0003.
Values may be sent and summed in bfloat16 or wider, within the bound.
A program may use at most 64 MiB of HBM per device.

```python
import math
import jax
import jax.numpy as jnp
from jax import lax

D = 8192
KV = 512
NR = 32
REP_TOK = 2048
TOKENS = 65536


def common_weights(key):
    return jnp.clip(jax.random.normal(key, (KV, D), jnp.float32), -5.0, 5.0)


def draw_anchor(key, part):
    base = common_weights(key)
    return base.astype(jnp.float32)


def draw_params(key, part):
    base = common_weights(key)
    key = jax.random.fold_in(key, 5)
    drift = 0.25 * jnp.clip(jax.random.normal(key, (NR, KV, D), jnp.float32), -5.0, 5.0)
    return (base[None] + drift).astype(jnp.bfloat16)


def levels(own_key, dims, pieces, smallest, largest):
    loudness = 1.0
    for position, parts in pieces:
        heights = jax.random.uniform(jax.random.fold_in(jax.random.fold_in(own_key, 6), position), (parts,), jnp.float32, smallest / len(pieces), largest / len(pieces))
        loudness = loudness * jnp.repeat(jnp.exp(heights), dims[position] // parts).reshape((-1,) + (1,) * (len(dims) - 1 - position))
    return loudness


def gaussian(key, shape, scale, limit, shards=(), dtype=jnp.bfloat16):
    factor_of = levels(key, shape, shards, -0.22, 0.18) if shards else 1.0
    result = jax.random.normal(key, shape, jnp.float32) * scale * factor_of
    return jnp.minimum(jnp.maximum(result, -limit), limit).astype(dtype)


def setup_inputs(seed: int = 0) -> dict:
    keys = jax.random.split(jax.random.key(seed), 9)
    return {
        "features": gaussian(keys[0], (TOKENS, D), 1.0, 6.0, ((0, 512),)),
        "cotangents": gaussian(keys[1], (TOKENS, KV), (REP_TOK ** -0.5), 0.13183594, ((0, 512),)),
        "params": draw_params(jax.random.fold_in(keys[8], 71), 0),
        "first_moment": gaussian(keys[3], (NR, KV, D), 1.0, 5.0, ((0, 32), (2, 16))),
        "second_moment": jnp.clip(jnp.exp(math.log(4.0) - 2.7725887 * jax.random.uniform(keys[4], (NR, KV, D), jnp.float32) ** levels(keys[4], (NR, KV, D), ((0, 32), (2, 16)), -0.2, 0.2)), 0.25, 4.0).astype(jnp.bfloat16),
        "anchor": draw_anchor(jax.random.fold_in(keys[8], 71), 0),
        "outer_momentum": gaussian(keys[6], (KV, D), 0.1, 0.5, ((0, 32), (1, 16)), jnp.float32),
        "step": jax.random.randint(keys[7], (1,), 1, 17).astype(jnp.int32),
    }


peak_rate = 0.25
warm_steps = 8.0
beta_one = 0.9
beta_two = 0.95
decay = 0.1
outer_rate = 0.7
outer_mu = 0.9
mix = 0.5

def reference(features, cotangents, params, first_moment, second_moment, anchor, outer_momentum, step):
    t_value = step[0].astype(jnp.float32)
    rate = peak_rate * jnp.minimum(1.0, t_value / warm_steps)
    fix_one = 1.0 - jnp.power(jnp.float32(beta_one), t_value)
    fix_two = 1.0 - jnp.power(jnp.float32(beta_two), t_value)
    feats = features.reshape(NR, REP_TOK, D)
    cots = cotangents.reshape(NR, REP_TOK, KV)

    def inner(items):
        feat, cot, weight, moment, second = items
        grad = jnp.dot(cot.T, feat, preferred_element_type=jnp.float32)
        weight = weight.astype(jnp.float32)
        moment_new = beta_one * moment.astype(jnp.float32) + (1.0 - beta_one) * grad
        second_new = beta_two * second.astype(jnp.float32) + (1.0 - beta_two) * grad * grad
        update = moment_new / fix_one / (jnp.sqrt(second_new / fix_two) + 1e-08)
        return weight - rate * (update + decay * weight)
    local = lax.map(inner, (feats, cots, params, first_moment, second_moment))
    delta = anchor - lax.optimization_barrier(jnp.sum(local, axis=0)) / NR
    momentum_next = outer_mu * outer_momentum + delta
    anchor_next = anchor - outer_rate * (delta + outer_mu * momentum_next)
    merged = mix * local + (1.0 - mix) * anchor_next[None]
    return (merged, momentum_next)
```

```python
import functools
import math

import jax
import jax.numpy as jnp
from jax import lax
from jax.experimental import pallas as pl
from jax.experimental.pallas import tpu as pltpu
from jax.sharding import PartitionSpec as P

peak_rate = 0.25
warm_steps = 8.0
beta_one = 0.9
beta_two = 0.95
decay = 0.1
outer_rate = 0.7
outer_mu = 0.9
mix = 0.5

NX, NY, NZ = 4, 4, 8
CHUNKS = 4
F32, BF16 = jnp.float32, jnp.bfloat16


def kernel(
    nx, nz, nc,
    feats, cots, params, first, second, anchor, outer_momentum, step,
    merged_out, momentum_out,
    cot_own, cot_t, cot_all, fbuf, par, mom1, mom2, anc, outer,
    own, keep, s1, sd, se, r1, rd, r2,
    loc, rcore, ssum, rz, tot, ry, nxt, mout, momn,
    in_sem, feat_sem, cs, cr, xs, xr, ys, yr, ks, kr, zs, zr, ls, lr, os,
):
    ny = NY
    rows, width = par.shape
    cw = width // nc
    half = rows // 2
    tokens = feats.shape[0]
    slab = rows // nz
    rep = lax.axis_index("replica")
    fs = lax.axis_index("fsdp")
    core = lax.rem(rep, 2)
    yl = lax.rem(lax.div(rep, 2), 2)
    z = lax.div(rep, 4)
    x = lax.div(fs, ny)
    q = lax.rem(fs, ny)

    def at_fsdp(xx, qq):
        return {"fsdp": xx * ny + qq}

    def at_rep(zz, ll, cc):
        return {"replica": zz * 4 + ll * 2 + cc}

    x_peer = [at_fsdp(lax.rem(x + d, nx), q) for d in range(nx)]
    y_up = at_fsdp(x, lax.rem(q + 1, ny))
    y_down = at_fsdp(x, lax.rem(q + ny - 1, ny))
    z_of = [lax.rem(z + d, nz) for d in range(nz)]
    z_peer = [at_rep(zz, yl, core) for zz in z_of]
    core_peer = at_rep(z, yl, 1 - core)
    lo_peer = at_rep(z, 1 - yl, core)

    loads = []
    for k, (src, dst) in enumerate(
        [
            (cots, cot_own),
            (params.at[0], par),
            (first.at[0], mom1),
            (second.at[0], mom2),
            (anchor, anc),
            (outer_momentum, outer),
        ]
    ):
        loads.append(pltpu.make_async_copy(src, dst, in_sem.at[k]))
        loads[-1].start()

    barrier = pltpu.get_barrier_semaphore()
    peers = x_peer[1:] + [y_up, y_down] + z_peer[1:] + [core_peer, lo_peer]
    for peer in peers:
        pl.semaphore_signal(
            barrier, inc=1, device_id=peer, device_id_type=pl.DeviceIdType.MESH
        )

    def owner_cols(xx, o):
        return pl.multiple_of((xx * ny + lax.rem(q + o, ny)) * width, width)

    own_feats = []
    for o in range(ny):
        own_feats.append(
            pltpu.make_async_copy(
                feats.at[:, pl.ds(owner_cols(x, o), width)],
                fbuf.at[o, 0],
                feat_sem.at[o],
            )
        )
        own_feats[-1].start()

    sent = []

    def send(src, dst, ssem, rsem, peer):
        copy = pltpu.make_async_remote_copy(
            src_ref=src,
            dst_ref=dst,
            send_sem=ssem,
            recv_sem=rsem,
            device_id=peer,
            device_id_type=pl.DeviceIdType.MESH,
        )
        copy.start()
        sent.append(copy)
        return copy

    loads[0].wait()
    cot_t[...] = cot_own[...].T

    pl.semaphore_wait(barrier, len(peers))

    cot_copies = [
        send(
            cot_t,
            cot_all.at[:, d * tokens : (d + 1) * tokens],
            cs.at[d],
            cr.at[d],
            x_peer[d],
        )
        for d in range(1, nx)
    ]
    cot_all[:, 0:tokens] = cot_t[...]

    x_copies = {}

    def x_send(c, o):
        x_copies[c, o] = [
            send(
                feats.at[:, pl.ds(owner_cols(lax.rem(x + d, nx), o) + c * cw, cw)],
                fbuf.at[o, d, :, c * cw : (c + 1) * cw],
                xs.at[c, o, d],
                xr.at[c, o, d],
                x_peer[d],
            )
            for d in range(1, nx)
        ]

    def x_send_chunk(c):
        for o in (2, 1, 3, 0):
            x_send(c, o)

    def partial(c, o):
        if c == 0:
            own_feats[o].wait()
        for copy in x_copies[c, o]:
            copy.wait_recv()
        block = fbuf[o, :, :, c * cw : (c + 1) * cw].reshape(nx * tokens, cw)
        return jnp.dot(cot_all[...], block, preferred_element_type=F32)

    y_copies = {}

    def far(c):
        s1[c] = partial(c, 2).astype(BF16)
        y_copies[c, "1a"] = send(s1.at[c, :half], r1.at[c, :half], ys.at[c, 0], yr.at[c, 0], y_down)
        y_copies[c, "1b"] = send(s1.at[c, half:], r1.at[c, half:], ys.at[c, 1], yr.at[c, 1], y_up)

    def near(c):
        up = partial(c, 1)
        sd[c, :half] = up[:half].astype(BF16)
        y_copies[c, "da"] = send(sd.at[c, :half], rd.at[c, :half], ys.at[c, 2], yr.at[c, 2], y_up)
        keep[c, half:] = up[half:]
        down = partial(c, 3)
        sd[c, half:] = down[half:].astype(BF16)
        y_copies[c, "db"] = send(sd.at[c, half:], rd.at[c, half:], ys.at[c, 3], yr.at[c, 3], y_down)
        keep[c, :half] = down[:half]

    def mine(c):
        own[c] = partial(c, 0)

    def relay(c):
        y_copies[c, "1a"].wait_recv()
        se[c, :half] = (keep[c, :half] + r1[c, :half].astype(F32)).astype(BF16)
        y_copies[c, "2a"] = send(se.at[c, :half], r2.at[c, :half], ys.at[c, 4], yr.at[c, 4], y_down)
        y_copies[c, "1b"].wait_recv()
        se[c, half:] = (keep[c, half:] + r1[c, half:].astype(F32)).astype(BF16)
        y_copies[c, "2b"] = send(se.at[c, half:], r2.at[c, half:], ys.at[c, 5], yr.at[c, 5], y_up)

    rep_copies = {}

    def adam(c):
        if c == 0:
            for k in (1, 2, 3):
                loads[k].wait()
        for name in ("da", "db", "2a", "2b"):
            y_copies[c, name].wait_recv()
        t_value = jnp.full((1, cw), step[0].astype(F32), F32)
        rate = peak_rate * jnp.minimum(1.0, t_value / warm_steps)
        inv_one = 1.0 / (1.0 - jnp.exp(t_value * math.log(beta_one)))
        inv_two = 1.0 / (1.0 - jnp.exp(t_value * math.log(beta_two)))
        cols = slice(c * cw, (c + 1) * cw)

        def body(k, carry):
            here = pl.ds(pl.multiple_of(k * slab, slab), slab)
            grad = own[c, here] + rd[c, here].astype(F32) + r2[c, here].astype(F32)
            weight = par[here, cols].astype(F32)
            m = beta_one * mom1[here, cols].astype(F32) + (1.0 - beta_one) * grad
            v = beta_two * mom2[here, cols].astype(F32) + (1.0 - beta_two) * grad * grad
            update = (m * inv_one) / (jnp.sqrt(v * inv_two) + 1e-08)
            new = weight - rate * (update + decay * weight)
            new = new.reshape(2, 2, slab // 4, cw)
            loc[c, 0, k] = new[:, 0]
            loc[c, 1, k] = new[:, 1]
            return carry

        lax.fori_loop(0, nz, body, 0)
        rep_copies[c, "core"] = send(
            loc.at[c, 1 - core], rcore.at[c], ks.at[c, 0], kr.at[c, 0], core_peer
        )

    def z_reduce(c):
        rep_copies[c, "core"].wait_recv()
        copies = []
        for d in list(range(1, nz)) + [0]:
            zz = z_of[d]
            ssum[c, zz] = loc[c, core, zz] + rcore[c, zz]
            if d:
                copies.append(
                    send(ssum.at[c, zz], rz.at[c, d], zs.at[c, 0, d], zr.at[c, 0, d], z_peer[d])
                )
        rep_copies[c, "z"] = copies

    def lo_reduce(c):
        total = ssum[c, z]
        for d, copy in enumerate(rep_copies[c, "z"], 1):
            copy.wait_recv()
            total = total + rz[c, d]
        tot[c] = total
        rep_copies[c, "lo"] = send(
            tot.at[c, 1 - yl], ry.at[c], ls.at[c, 0], lr.at[c, 0], lo_peer
        )

    def outer_step(c):
        if c == 0:
            loads[4].wait()
            loads[5].wait()
        cols = slice(c * cw, (c + 1) * cw)
        rep_copies[c, "lo"].wait_recv()
        old = anc[:, cols]
        delta = old - (tot[c, yl] + ry[c]) * (1.0 / (4 * nz))
        momentum = outer_mu * outer[:, cols] + delta
        momn[:, cols] = momentum
        nxt[c, core, z, yl] = old - outer_rate * (delta + outer_mu * momentum)
        piece = nxt.at[c, core, z, yl]
        rep_copies[c, "lo2"] = send(piece, piece, ls.at[c, 1], lr.at[c, 1], lo_peer)

    def z_gather(c):
        rep_copies[c, "lo2"].wait_recv()
        piece = nxt.at[c, core, z]
        rep_copies[c, "z2"] = [
            send(piece, piece, zs.at[c, 1, d], zr.at[c, 1, d], z_peer[d])
            for d in range(1, nz)
        ]

    def core_gather(c):
        for copy in rep_copies[c, "z2"]:
            copy.wait_recv()
        piece = nxt.at[c, core]
        rep_copies[c, "core2"] = send(piece, piece, ks.at[c, 1], kr.at[c, 1], core_peer)

    out_copies = []

    def merge(c):
        rep_copies[c, "core2"].wait_recv()

        def body(k, carry):
            here = pl.ds(pl.multiple_of(k * slab, slab), slab)
            both = [mix * loc[c, j, k] + (1.0 - mix) * nxt[c, j, k] for j in (0, 1)]
            mout[c, here] = jnp.stack(both, axis=1).reshape(slab, cw)
            return carry

        lax.fori_loop(0, nz, body, 0)
        copy = pltpu.make_async_copy(
            mout.at[c], merged_out.at[0, :, c * cw : (c + 1) * cw], os.at[c]
        )
        copy.start()
        out_copies.append(copy)

    x_send_chunk(0)
    if nc > 1:
        x_send_chunk(1)
    for copy in cot_copies:
        copy.wait_recv()
    stages = [
        ("far", 0, far), ("x", 0, None), ("near", 0, near), ("mine", 0, mine),
        ("lo_reduce", 2, lo_reduce), ("core_gather", 3, core_gather),
        ("adam", 1, adam), ("outer", 2, outer_step), ("relay", 0, relay),
        ("z_reduce", 1, z_reduce), ("z_gather", 2, z_gather), ("merge", 3, merge),
    ]
    for k in range(nc + 3):
        for name, lag, stage in stages:
            c = k - lag
            if not 0 <= c < nc:
                continue
            if name == "x":
                if c + 2 < nc:
                    x_send_chunk(c + 2)
            else:
                stage(c)

    momentum_copy = pltpu.make_async_copy(momn, momentum_out, os.at[nc])
    momentum_copy.start()
    for copy in sent:
        copy.wait_send()
    for copy in out_copies:
        copy.wait()
    momentum_copy.wait()


def per_device(features, cotangents, params, first, second, anchor, outer_momentum, step, *, nx, nz, nc):
    tokens = features.shape[0]
    rows, width = params.shape[1:]
    cw = width // nc
    piece = anchor.shape[0]
    hbm = pl.BlockSpec(memory_space=pl.ANY)
    dma = pltpu.SemaphoreType.DMA
    return pl.pallas_call(
        functools.partial(kernel, nx, nz, nc),
        out_shape=(
            jax.ShapeDtypeStruct((1, rows, width), F32),
            jax.ShapeDtypeStruct((piece, width), F32),
        ),
        in_specs=[hbm] * 7 + [pl.BlockSpec(memory_space=pltpu.SMEM)],
        out_specs=(hbm, hbm),
        scratch_shapes=[
            pltpu.VMEM((tokens, rows), BF16),
            pltpu.VMEM((rows, tokens), BF16),
            pltpu.VMEM((rows, nx * tokens), BF16),
            pltpu.VMEM((NY, nx, tokens, width), BF16),
            pltpu.VMEM((rows, width), BF16),
            pltpu.VMEM((rows, width), BF16),
            pltpu.VMEM((rows, width), BF16),
            pltpu.VMEM((piece, width), F32),
            pltpu.VMEM((piece, width), F32),
            pltpu.VMEM((nc, rows, cw), F32),
            pltpu.VMEM((nc, rows, cw), F32),
            pltpu.VMEM((nc, rows, cw), BF16),
            pltpu.VMEM((nc, rows, cw), BF16),
            pltpu.VMEM((nc, rows, cw), BF16),
            pltpu.VMEM((nc, rows, cw), BF16),
            pltpu.VMEM((nc, rows, cw), BF16),
            pltpu.VMEM((nc, rows, cw), BF16),
            pltpu.VMEM((nc, 2, nz, 2, piece, cw), F32),
            pltpu.VMEM((nc, nz, 2, piece, cw), F32),
            pltpu.VMEM((nc, nz, 2, piece, cw), F32),
            pltpu.VMEM((nc, nz, 2, piece, cw), F32),
            pltpu.VMEM((nc, 2, piece, cw), F32),
            pltpu.VMEM((nc, piece, cw), F32),
            pltpu.VMEM((nc, 2, nz, 2, piece, cw), F32),
            pltpu.VMEM((nc, rows, cw), F32),
            pltpu.VMEM((piece, width), F32),
            dma((6,)), dma((NY,)),
            dma((nx,)), dma((nx,)),
            dma((nc, NY, nx)), dma((nc, NY, nx)),
            dma((nc, 6)), dma((nc, 6)),
            dma((nc, 2)), dma((nc, 2)),
            dma((nc, 2, nz)), dma((nc, 2, nz)),
            dma((nc, 2)), dma((nc, 2)),
            dma((nc + 1,)),
        ],
        compiler_params=pltpu.CompilerParams(
            collective_id=0, has_side_effects=True, vmem_limit_bytes=48 * 1024 * 1024
        ),
    )(features, cotangents, params, first, second, anchor, outer_momentum, step)


def build(mesh, nx, nz, nc):
    in_specs = (
        P(("replica", "fsdp"), None),
        P(("replica", "fsdp"), None),
        P("replica", None, "fsdp"),
        P("replica", None, "fsdp"),
        P("replica", None, "fsdp"),
        P("replica", "fsdp"),
        P("replica", "fsdp"),
        P(),
    )
    out_specs = (P("replica", None, "fsdp"), P("replica", "fsdp"))
    return jax.shard_map(
        functools.partial(per_device, nx=nx, nz=nz, nc=nc),
        mesh=mesh, in_specs=in_specs, out_specs=out_specs, check_vma=False,
    )


def solution(mesh):
    return build(mesh, NX, NZ, CHUNKS)
```

```python
import functools
import math

import jax
import jax.numpy as jnp
from jax import lax
from jax.experimental import pallas as pl
from jax.experimental.pallas import tpu as pltpu
from jax.sharding import PartitionSpec as P

peak_rate = 0.25
warm_steps = 8.0
beta_one = 0.9
beta_two = 0.95
decay = 0.1
outer_rate = 0.7
outer_mu = 0.9
mix = 0.5

NX, NY, NZ = 4, 4, 8
CHUNKS = 4
AHEAD = 2
F32, BF16 = jnp.float32, jnp.bfloat16


def kernel(
    nx, nz, nc,
    feats, cots, params, first, second, anchor, outer_momentum, step,
    merged_out, momentum_out,
    cot_own, cot_t, cot_all, fbuf, par, mom1, mom2, anc, outer,
    own, keep, s1, sd, se, r1, rd, r2,
    loc, rcore, ssum, rz, tot, ry, nxt, mout, momn,
    step_v, in_sem, feat_sem, cs, cr, xs, xr, ys, yr, ks, kr, os_, zs, zr, ls, lr, os,
):
    ny = NY
    rows, width = par.shape
    cw = width // nc
    half = rows // 2
    tokens = feats.shape[0]
    slab = rows // nz
    rep = lax.axis_index("replica")
    fs = lax.axis_index("fsdp")
    core = lax.rem(rep, 2)
    yl = lax.rem(lax.div(rep, 2), 2)
    z = lax.div(rep, 4)
    x = lax.div(fs, ny)
    q = lax.rem(fs, ny)

    def at_fsdp(xx, qq):
        return {"fsdp": xx * ny + qq}

    def at_rep(zz, ll, cc):
        return {"replica": zz * 4 + ll * 2 + cc}

    x_peer = [at_fsdp(lax.rem(x + d, nx), q) for d in range(nx)]
    y_up = at_fsdp(x, lax.rem(q + 1, ny))
    y_down = at_fsdp(x, lax.rem(q + ny - 1, ny))
    z_of = [lax.rem(z + d, nz) for d in range(nz)]
    z_peer = [[at_rep(zz, yl, core), at_rep(zz, 1 - yl, core)] for zz in z_of]
    core_peer = at_rep(z, yl, 1 - core)
    lo_peer = z_peer[0][1]

    loads = []
    for k, (src, dst) in enumerate(
        [
            (cots, cot_own),
            (params.at[0], par),
            (first.at[0], mom1),
            (second.at[0], mom2),
            (anchor, anc.at[yl]),
            (outer_momentum, outer.at[yl]),
            (step, step_v),
        ]
    ):
        loads.append(pltpu.make_async_copy(src, dst, in_sem.at[k]))
        loads[-1].start()

    barrier = pltpu.get_barrier_semaphore()
    peers = x_peer[1:] + [y_up, y_down, core_peer] + [p for d in range(nz) for p in z_peer[d]][1:]
    for peer in peers:
        pl.semaphore_signal(
            barrier, inc=1, device_id=peer, device_id_type=pl.DeviceIdType.MESH
        )

    def owner_cols(xx, o):
        return pl.multiple_of((xx * ny + lax.rem(q + o, ny)) * width, width)

    own_feats = []
    for o in range(ny):
        own_feats.append(
            pltpu.make_async_copy(
                feats.at[:, pl.ds(owner_cols(x, o), width)],
                fbuf.at[o, 0],
                feat_sem.at[o],
            )
        )
        own_feats[-1].start()

    sent = []

    def send(src, dst, ssem, rsem, peer):
        copy = pltpu.make_async_remote_copy(
            src_ref=src,
            dst_ref=dst,
            send_sem=ssem,
            recv_sem=rsem,
            device_id=peer,
            device_id_type=pl.DeviceIdType.MESH,
        )
        copy.start()
        sent.append(copy)
        return copy

    loads[0].wait()
    cot_t[...] = cot_own[...].T

    pl.semaphore_wait(barrier, len(peers))

    cot_copies = {}

    def cot_send(h):
        some = slice(h * half, (h + 1) * half)
        cot_copies[h] = [
            send(
                cot_t.at[some],
                cot_all.at[some, d * tokens : (d + 1) * tokens],
                cs.at[h, d],
                cr.at[h, d],
                x_peer[d],
            )
            for d in range(1, nx)
        ]

    cot_all[:, 0:tokens] = cot_t[...]
    outer_copies = [
        send(src, dst.at[yl], os_.at[0, k], os_.at[1, k], lo_peer)
        for k, (src, dst) in enumerate([(anchor, anc), (outer_momentum, outer)])
    ]

    x_copies = {}

    def x_send(c, o):
        x_copies[c, o] = [
            send(
                feats.at[:, pl.ds(owner_cols(lax.rem(x + d, nx), o) + c * cw, cw)],
                fbuf.at[o, d, :, c * cw : (c + 1) * cw],
                xs.at[c, o, d],
                xr.at[c, o, d],
                x_peer[d],
            )
            for d in range(1, nx)
        ]

    x_order = [(c + 1 if o == 2 else c, o) for c in range(-1, nc) for o in (2, 1, 3, 0)]
    x_order = [(c, o) for c, o in x_order if 0 <= c < nc]
    x_done = [0]

    def x_ahead(c, o, more=AHEAD):
        upto = min(x_order.index((c, o)) + 1 + more, len(x_order))
        for at in range(x_done[0], upto):
            x_send(*x_order[at])
        x_done[0] = max(x_done[0], upto)

    def block(c, o):
        x_ahead(c, o)
        if c == 0:
            own_feats[o].wait()
        for copy in x_copies[c, o]:
            copy.wait_recv()
        return fbuf[o, :, :, c * cw : (c + 1) * cw].reshape(nx * tokens, cw)

    halves = (slice(0, half), slice(half, rows))

    def dot(h, cols):
        for copy in cot_copies.pop(h, []):
            copy.wait_recv()
        return jnp.dot(cot_all[halves[h]], cols, preferred_element_type=F32)

    y_copies = {}

    def y_send(c, k, h, src, dst, peer):
        y_copies[c, k] = send(
            src.at[c, halves[h]], dst.at[c, halves[h]], ys.at[c, k], yr.at[c, k], peer
        )

    def far(c):
        cols = block(c, 2)
        for h, peer in ((0, y_down), (1, y_up)):
            s1[c, halves[h]] = dot(h, cols).astype(BF16)
            y_send(c, h, h, s1, r1, peer)

    def near(c):
        cols = block(c, 1)
        sd[c, :half] = dot(0, cols).astype(BF16)
        y_send(c, 2, 0, sd, rd, y_up)
        keep[c, half:] = dot(1, cols)
        cols = block(c, 3)
        sd[c, half:] = dot(1, cols).astype(BF16)
        y_send(c, 3, 1, sd, rd, y_down)
        keep[c, :half] = dot(0, cols)

    def relay(c):
        for h, peer in ((0, y_down), (1, y_up)):
            y_copies[c, h].wait_recv()
            se[c, halves[h]] = (keep[c, halves[h]] + r1[c, halves[h]].astype(F32)).astype(BF16)
            y_send(c, 4 + h, h, se, r2, peer)

    def mine(c):
        cols = block(c, 0)
        for h in (0, 1):
            own[c, halves[h]] = dot(h, cols)

    rep_copies = {}

    def adam(c):
        if c == 0:
            for k in (1, 2, 3, 6):
                loads[k].wait()
        for k in (2, 3, 4, 5):
            y_copies[c, k].wait_recv()
        t_value = jnp.full((1, cw), step_v[0].astype(F32), F32)
        rate = peak_rate * jnp.minimum(1.0, t_value / warm_steps)
        inv_one = 1.0 / (1.0 - jnp.exp(t_value * math.log(beta_one)))
        inv_two = 1.0 / (1.0 - jnp.exp(t_value * math.log(beta_two)))
        cols = slice(c * cw, (c + 1) * cw)

        def body(k, carry):
            here = pl.ds(pl.multiple_of(k * slab, slab), slab)
            grad = own[c, here] + rd[c, here].astype(F32) + r2[c, here].astype(F32)
            weight = par[here, cols].astype(F32)
            m = beta_one * mom1[here, cols].astype(F32) + (1.0 - beta_one) * grad
            v = beta_two * mom2[here, cols].astype(F32) + (1.0 - beta_two) * grad * grad
            update = (m * inv_one) / (jnp.sqrt(v * inv_two) + 1e-08)
            new = weight - rate * (update + decay * weight)
            new = new.reshape(2, 2, slab // 4, cw)
            loc[c, 0, k] = new[:, 0]
            loc[c, 1, k] = new[:, 1]
            return carry

        lax.fori_loop(0, nz, body, 0)
        rep_copies[c, "core"] = send(
            loc.at[c, 1 - core], rcore.at[c], ks.at[c, 0], kr.at[c, 0], core_peer
        )

    straight = [c == nc - 1 for c in range(nc)]

    def z_reduce(c):
        rep_copies[c, "core"].wait_recv()
        copies = []
        for d in list(range(1, nz)) + [0]:
            zz = z_of[d]
            ssum[c, zz] = loc[c, core, zz] + rcore[c, zz]
            if straight[c]:
                for e in (0, 1):
                    if d or e:
                        lo = 1 - yl if e else yl
                        copies.append(
                            send(ssum.at[c, zz, lo], rz.at[c, d, e], zs.at[c, 0, d, e], zr.at[c, 0, d, e], z_peer[d][e])
                        )
            elif d:
                copies.append(
                    send(ssum.at[c, zz], rz.at[c, d], zs.at[c, 0, d, 0], zr.at[c, 0, d, 0], z_peer[d][0])
                )
        rep_copies[c, "z"] = copies

    def lo_reduce(c):
        for copy in rep_copies[c, "z"]:
            copy.wait_recv()
        if straight[c]:
            total = ssum[c, z, yl] + rz[c, 0, 1]
            for d in range(1, nz):
                total = total + (rz[c, d, 0] + rz[c, d, 1])
            tot[c, 0] = total
        else:
            total = ssum[c, z]
            for d in range(1, nz):
                total = total + rz[c, d]
            tot[c] = total
            rep_copies[c, "lo"] = send(tot.at[c], ry.at[c], ls.at[c], lr.at[c], lo_peer)

    def outer_step(c):
        cols = slice(c * cw, (c + 1) * cw)
        if straight[c]:
            total, rows_of = tot[c, 0], yl
        else:
            rep_copies[c, "lo"].wait_recv()
            total, rows_of = tot[c] + ry[c], slice(None)
        old = anc[rows_of, :, cols]
        delta = old - total * (1.0 / (4 * nz))
        momentum = outer_mu * outer[rows_of, :, cols] + delta
        nxt[c, core, z, rows_of] = old - outer_rate * (delta + outer_mu * momentum)
        piece = nxt.at[c, core, z, yl] if straight[c] else nxt.at[c, core, z]
        rep_copies[c, "z2"] = [
            send(piece, piece, zs.at[c, 1, d, e], zr.at[c, 1, d, e], z_peer[d][e])
            for d in range(nz)
            for e in ((0, 1) if straight[c] else (0,))
            if d or e
        ]
        momn[rows_of, :, cols] = momentum

    def core_gather(c):
        for copy in rep_copies[c, "z2"]:
            copy.wait_recv()
        piece = nxt.at[c, core]
        rep_copies[c, "core2"] = send(piece, piece, ks.at[c, 1], kr.at[c, 1], core_peer)

    out_copies = []

    def merge(c):
        rep_copies[c, "core2"].wait_recv()

        def body(k, carry):
            here = pl.ds(pl.multiple_of(k * slab, slab), slab)
            both = [mix * loc[c, j, k] + (1.0 - mix) * nxt[c, j, k] for j in (0, 1)]
            mout[c, here] = jnp.stack(both, axis=1).reshape(slab, cw)
            return carry

        lax.fori_loop(0, nz, body, 0)
        copy = pltpu.make_async_copy(
            mout.at[c], merged_out.at[0, :, c * cw : (c + 1) * cw], os.at[c]
        )
        copy.start()
        out_copies.append(copy)

    cot_send(0)
    x_ahead(*x_order[0])
    cot_send(1)
    far(0)
    for k in range(nc + 1):
        if k + 1 < nc:
            far(k + 1)
        if k < nc:
            near(k)
            relay(k)
            mine(k)
        if k + 1 < nc:
            x_ahead(k + 1, 0, 0)
        if k == 2:
            for copy in loads[4:6]:
                copy.wait()
            for copy in outer_copies:
                copy.wait_recv()
        stages = [(outer_step, 3), (core_gather, 4), (lo_reduce, 2), (merge, 4), (adam, 1), (z_reduce, 1)]
        for stage, lag in stages:
            if 0 <= k - lag < nc:
                stage(k - lag)
    c = nc - 1
    for stage, lag in [
        (outer_step, 1), (core_gather, 2), (merge, 2), (lo_reduce, 0), (outer_step, 0),
        (core_gather, 1), (merge, 1), (core_gather, 0), (merge, 0),
    ]:
        stage(c - lag)

    momentum_copy = pltpu.make_async_copy(momn.at[yl], momentum_out, os.at[nc])
    momentum_copy.start()
    for copy in sent:
        copy.wait_send()
    for copy in out_copies:
        copy.wait()
    momentum_copy.wait()


def per_device(features, cotangents, params, first, second, anchor, outer_momentum, step, *, nx, nz, nc):
    tokens = features.shape[0]
    rows, width = params.shape[1:]
    cw = width // nc
    piece = anchor.shape[0]
    hbm = pl.BlockSpec(memory_space=pl.ANY)
    dma = pltpu.SemaphoreType.DMA
    operands = [
        pltpu.with_memory_space_constraint(a, pltpu.HBM)
        for a in (features, cotangents, params, first, second, anchor, outer_momentum)
    ]
    return pl.pallas_call(
        functools.partial(kernel, nx, nz, nc),
        out_shape=(
            jax.ShapeDtypeStruct((1, rows, width), F32),
            jax.ShapeDtypeStruct((piece, width), F32),
        ),
        in_specs=[hbm] * 8,
        out_specs=(hbm, hbm),
        scratch_shapes=[
            pltpu.VMEM((tokens, rows), BF16),
            pltpu.VMEM((rows, tokens), BF16),
            pltpu.VMEM((rows, nx * tokens), BF16),
            pltpu.VMEM((NY, nx, tokens, width), BF16),
            pltpu.VMEM((rows, width), BF16),
            pltpu.VMEM((rows, width), BF16),
            pltpu.VMEM((rows, width), BF16),
            pltpu.VMEM((2, piece, width), F32),
            pltpu.VMEM((2, piece, width), F32),
            pltpu.VMEM((nc, rows, cw), F32),
            pltpu.VMEM((nc, rows, cw), F32),
            pltpu.VMEM((nc, rows, cw), BF16),
            pltpu.VMEM((nc, rows, cw), BF16),
            pltpu.VMEM((nc, rows, cw), BF16),
            pltpu.VMEM((nc, rows, cw), BF16),
            pltpu.VMEM((nc, rows, cw), BF16),
            pltpu.VMEM((nc, rows, cw), BF16),
            pltpu.VMEM((nc, 2, nz, 2, piece, cw), F32),
            pltpu.VMEM((nc, nz, 2, piece, cw), F32),
            pltpu.VMEM((nc, nz, 2, piece, cw), F32),
            pltpu.VMEM((nc, nz, 2, piece, cw), F32),
            pltpu.VMEM((nc, 2, piece, cw), F32),
            pltpu.VMEM((nc, 2, piece, cw), F32),
            pltpu.VMEM((nc, 2, nz, 2, piece, cw), F32),
            pltpu.VMEM((nc, rows, cw), F32),
            pltpu.VMEM((2, piece, width), F32),
            pltpu.SMEM((1,), jnp.int32),
            dma((7,)), dma((NY,)),
            dma((2, nx)), dma((2, nx)),
            dma((nc, NY, nx)), dma((nc, NY, nx)),
            dma((nc, 6)), dma((nc, 6)),
            dma((nc, 2)), dma((nc, 2)),
            dma((2, 2)),
            dma((nc, 2, nz, 2)), dma((nc, 2, nz, 2)),
            dma((nc,)), dma((nc,)),
            dma((nc + 1,)),
        ],
        compiler_params=pltpu.CompilerParams(
            collective_id=0, has_side_effects=True, vmem_limit_bytes=48 * 1024 * 1024
        ),
    )(*operands, step)


def build(mesh, nx, nz, nc):
    in_specs = (
        P(("replica", "fsdp"), None),
        P(("replica", "fsdp"), None),
        P("replica", None, "fsdp"),
        P("replica", None, "fsdp"),
        P("replica", None, "fsdp"),
        P("replica", "fsdp"),
        P("replica", "fsdp"),
        P(),
    )
    out_specs = (P("replica", None, "fsdp"), P("replica", "fsdp"))
    return jax.shard_map(
        functools.partial(per_device, nx=nx, nz=nz, nc=nc),
        mesh=mesh, in_specs=in_specs, out_specs=out_specs, check_vma=False,
    )


def solution(mesh):
    return build(mesh, NX, NZ, CHUNKS)
```

```python
import functools
import math

import jax
import jax.numpy as jnp
from jax import lax
from jax.experimental import pallas as pl
from jax.experimental.pallas import tpu as pltpu
from jax.sharding import PartitionSpec as P

peak_rate = 0.25
warm_steps = 8.0
beta_one = 0.9
beta_two = 0.95
decay = 0.1
outer_rate = 0.7
outer_mu = 0.9
mix = 0.5

NX, NY, NZ = 4, 4, 8
CHUNKS = 4
SUB = 8
F32, BF16 = jnp.float32, jnp.bfloat16


def kernel(
    nx, nz, nc, y_units, r_units, straight,
    feats, cots, params, first, second, anchor, outer_momentum, step,
    merged_out, momentum_out,
    cot_own, cot_t, cot_all, fbuf, par, mom1, mom2, anc, outer,
    own, keep, s1, sd, se, r1, rd, r2,
    loc, rcore, ssum, rz, tot, ry, nxt, mout, momn,
    step_v, in_sem, feat_sem, cs, cr, xs, xr, ys, yr, ks, kr, os_, zs, zr, ls, lr, os,
):
    ny = NY
    rows, width = par.shape
    cw = width // nc
    tokens = feats.shape[0]
    slab = rows // nz
    part = rows // 2
    quarter = rows // 4
    rep = lax.axis_index("replica")
    fs = lax.axis_index("fsdp")
    core = lax.rem(rep, 2)
    yl = lax.rem(lax.div(rep, 2), 2)
    z = lax.div(rep, 4)
    x = lax.div(fs, ny)
    q = lax.rem(fs, ny)

    def at_fsdp(xx, qq):
        return {"fsdp": xx * ny + qq}

    def at_rep(zz, ll, cc):
        return {"replica": zz * 4 + ll * 2 + cc}

    x_peer = [at_fsdp(lax.rem(x + d, nx), q) for d in range(nx)]
    y_up = at_fsdp(x, lax.rem(q + 1, ny))
    y_down = at_fsdp(x, lax.rem(q + ny - 1, ny))
    z_of = [lax.rem(z + d, nz) for d in range(nz)]
    z_peer = [[at_rep(zz, yl, core), at_rep(zz, 1 - yl, core)] for zz in z_of]
    core_peer = at_rep(z, yl, 1 - core)
    lo_peer = z_peer[0][1]

    loads = []
    for k, (src, dst) in enumerate(
        [
            (cots, cot_own),
            (params.at[0], par),
            (first.at[0], mom1),
            (second.at[0], mom2),
            (anchor, anc.at[yl]),
            (outer_momentum, outer.at[yl]),
            (step, step_v),
        ]
    ):
        loads.append(pltpu.make_async_copy(src, dst, in_sem.at[k]))
        loads[-1].start()

    barrier = pltpu.get_barrier_semaphore()
    peers = x_peer[1:] + [y_up, y_down, core_peer] + [p for d in range(nz) for p in z_peer[d]][1:]
    for peer in peers:
        pl.semaphore_signal(
            barrier, inc=1, device_id=peer, device_id_type=pl.DeviceIdType.MESH
        )

    def owner_cols(xx, o):
        return pl.multiple_of((xx * ny + lax.rem(q + o, ny)) * width, width)

    own_feats = []
    for o in range(ny):
        own_feats.append(
            pltpu.make_async_copy(
                feats.at[:, pl.ds(owner_cols(x, o), width)],
                fbuf.at[o, 0],
                feat_sem.at[o],
            )
        )
        own_feats[-1].start()

    sent = []

    def send(src, dst, ssem, rsem, peer):
        copy = pltpu.make_async_remote_copy(
            src_ref=src,
            dst_ref=dst,
            send_sem=ssem,
            recv_sem=rsem,
            device_id=peer,
            device_id_type=pl.DeviceIdType.MESH,
        )
        copy.start()
        sent.append(copy)
        return copy

    loads[0].wait()
    turned = cot_own[...].astype(F32).T.reshape(4 * nz, 2, SUB, tokens)
    for u in (0, 1):
        cot_t[u * part : (u + 1) * part] = turned[:, u].reshape(part, tokens).astype(BF16)

    pl.semaphore_wait(barrier, len(peers))

    cot_copies = {}

    def cot_send(k):
        some = slice(k * quarter, (k + 1) * quarter)
        cot_copies[k] = [
            send(
                cot_t.at[some],
                cot_all.at[some, d * tokens : (d + 1) * tokens],
                cs.at[k, d - 1],
                cr.at[k, d - 1],
                x_peer[d],
            )
            for d in range(1, nx)
        ]

    x_copies = {}

    def x_send(c, o):
        x_copies[c, o] = [
            send(
                feats.at[:, pl.ds(owner_cols(lax.rem(x + d, nx), o) + c * cw, cw)],
                fbuf.at[o, d, :, c * cw : (c + 1) * cw],
                xs.at[c, o, d - 1],
                xr.at[c, o, d - 1],
                x_peer[d],
            )
            for d in range(1, nx)
        ]

    x_order = []
    for i, (c, lo, hi) in enumerate(y_units):
        ahead = y_units[i + 1 : i + 2] if i else y_units[:2]
        uses = [(a[0], 2) for a in ahead] + [(c, o) for o in (1, 3, 0)]
        for use in uses:
            if use not in x_order:
                x_order.append(use)
    x_done, cots_done = [0], [0]

    def x_upto(n):
        for use in x_order[x_done[0] : n]:
            x_send(*use)
        x_done[0] = max(x_done[0], n)

    def cots_upto(n):
        for k in range(cots_done[0], n):
            cot_send(k)
        cots_done[0] = max(cots_done[0], n)

    arrived = set()

    def block(c, o):
        x_upto(x_order.index((c, o)) + 1)
        if (c, o) not in arrived:
            arrived.add((c, o))
            if c == 0:
                own_feats[o].wait()
            for copy in x_copies[c, o]:
                copy.wait_recv()
        return fbuf[o, :, :, c * cw : (c + 1) * cw].reshape(nx * tokens, cw)

    def dot(lo, hi, cols):
        for k in range(lo // quarter, -(-hi // quarter)):
            for copy in cot_copies.pop(k, []):
                copy.wait_recv()
        return jnp.dot(cot_all[lo:hi], cols, preferred_element_type=F32)

    y_copies = {}

    def y_halves(i):
        c, lo, hi = y_units[i]
        mid = (lo + hi) // 2
        return c, (lo, mid), (mid, hi)

    def y_send(i, k, c, some, src, dst, peer):
        here = slice(*some)
        y_copies[i, k] = send(
            src.at[c, here], dst.at[c, here], ys.at[i, k], yr.at[i, k], peer
        )

    def far(i):
        c, a, b = y_halves(i)
        cols = block(c, 2)
        for k, some, peer in ((0, a, y_down), (1, b, y_up)):
            s1[c, slice(*some)] = dot(*some, cols).astype(BF16)
            y_send(i, k, c, some, s1, r1, peer)

    def near(i):
        c, a, b = y_halves(i)
        for k, o, direct, kept, peer in ((2, 1, a, b, y_up), (3, 3, b, a, y_down)):
            cols = block(c, o)
            sd[c, slice(*direct)] = dot(*direct, cols).astype(BF16)
            y_send(i, k, c, direct, sd, rd, peer)
            keep[c, slice(*kept)] = dot(*kept, cols)

    def relay(i):
        c, a, b = y_halves(i)
        for k, some, peer in ((0, a, y_down), (1, b, y_up)):
            here = slice(*some)
            y_copies[i, k].wait_recv()
            se[c, here] = (keep[c, here] + r1[c, here].astype(F32)).astype(BF16)
            y_send(i, 4 + k, c, some, se, r2, peer)

    def mine(c):
        cols = block(c, 0)
        for h in (0, 1):
            own[c, h * part : (h + 1) * part] = dot(h * part, (h + 1) * part, cols)

    rep_copies = {}

    def halves_of(j):
        c, us = r_units[j]
        return c, us, (slice(None) if len(us) == 2 else us[0])

    def adam(j):
        c, us, at = halves_of(j)
        if j == 0:
            for k in (1, 2, 3, 6):
                loads[k].wait()
        for i, (cc, lo, hi) in enumerate(y_units):
            if cc == c and any(lo < (u + 1) * part and u * part < hi for u in us):
                for k in (2, 3, 4, 5):
                    y_copies[i, k].wait_recv()
        t_value = jnp.full((1, cw), step_v[0].astype(F32), F32)
        rate = peak_rate * jnp.minimum(1.0, t_value / warm_steps)
        inv_one = 1.0 / (1.0 - jnp.exp(t_value * math.log(beta_one)))
        inv_two = 1.0 / (1.0 - jnp.exp(t_value * math.log(beta_two)))
        cols = slice(c * cw, (c + 1) * cw)

        def body(k, carry):
            here = pl.ds(pl.multiple_of(k * slab, slab), slab)
            for u in us:
                def rows_of(ref):
                    strip = ref[here, cols].astype(F32).reshape(4, 2, SUB, cw)
                    return strip[:, u].reshape(4 * SUB, cw)

                there = pl.ds(pl.multiple_of(u * part + k * (slab // 2), slab // 2), slab // 2)
                grad = own[c, there] + rd[c, there].astype(F32) + r2[c, there].astype(F32)
                weight = rows_of(par)
                m = beta_one * rows_of(mom1) + (1.0 - beta_one) * grad
                v = beta_two * rows_of(mom2) + (1.0 - beta_two) * grad * grad
                update = (m * inv_one) / (jnp.sqrt(v * inv_two) + 1e-08)
                new = weight - rate * (update + decay * weight)
                new = new.reshape(2, 2, SUB, cw)
                loc[c, 0, k, u] = new[:, 0]
                loc[c, 1, k, u] = new[:, 1]
            return carry

        lax.fori_loop(0, nz, body, 0)
        rep_copies[j, "core"] = send(
            loc.at[c, 1 - core, :, at], rcore.at[c, :, at], ks.at[j, 0], kr.at[j, 0], core_peer
        )

    z_first = [0]
    for flag in straight:
        z_first.append(z_first[-1] + (4 if flag else 2) * nz)

    def z_send(j, stage, d, e, src, dst):
        at = z_first[j] + ((stage * nz + d) * 2 + e if straight[j] else stage * nz + d)
        return send(src, dst, zs.at[at], zr.at[at], z_peer[d][e])

    def z_reduce(j):
        c, us, at = halves_of(j)
        rep_copies[j, "core"].wait_recv()
        copies = []
        for d in sorted(range(nz), key=lambda d: -min(d, nz - d)):
            zz = z_of[d]
            ssum[c, zz, at] = loc[c, core, zz, at] + rcore[c, zz, at]
            for e in (0, 1) if straight[j] else (0,):
                if d or e:
                    lo = (1 - yl if e else yl) if straight[j] else slice(None)
                    to = e if straight[j] else slice(None)
                    copies.append(
                        z_send(j, 0, d, e, ssum.at[c, zz, at, lo], rz.at[c, d, at, to])
                    )
        rep_copies[j, "z"] = copies

    def lo_reduce(j):
        c, us, at = halves_of(j)
        for copy in rep_copies[j, "z"]:
            copy.wait_recv()
        if straight[j]:
            total = ssum[c, z, at, yl] + rz[c, 0, at, 1]
            for d in range(1, nz):
                total = total + (rz[c, d, at, 0] + rz[c, d, at, 1])
            tot[c, at, 0] = total
        else:
            total = ssum[c, z, at]
            for d in range(1, nz):
                total = total + rz[c, d, at]
            tot[c, at] = total
            rep_copies[j, "lo"] = send(tot.at[c, at], ry.at[c, at], ls.at[j], lr.at[j], lo_peer)

    def outer_step(j):
        c, us, at = halves_of(j)
        cols = slice(c * cw, (c + 1) * cw)
        if not straight[j]:
            rep_copies[j, "lo"].wait_recv()
        for u in us:
            some = slice(u * SUB, (u + 1) * SUB)
            if straight[j]:
                total, who = tot[c, u, 0], yl
            else:
                total, who = tot[c, u] + ry[c, u], slice(None)
            old = anc[who, some, cols]
            delta = old - total * (1.0 / (4 * nz))
            momentum = outer_mu * outer[who, some, cols] + delta
            nxt[c, core, z, u, who] = old - outer_rate * (delta + outer_mu * momentum)
            momn[who, some, cols] = momentum
        piece = nxt.at[c, core, z, at, yl] if straight[j] else nxt.at[c, core, z, at]
        rep_copies[j, "z2"] = [
            z_send(j, 1, d, e, piece, piece)
            for d in sorted(range(nz), key=lambda d: -min(d, nz - d))
            for e in ((0, 1) if straight[j] else (0,))
            if d or e
        ]

    def core_gather(j):
        c, us, at = halves_of(j)
        for copy in rep_copies[j, "z2"]:
            copy.wait_recv()
        piece = nxt.at[c, core, :, at]
        rep_copies[j, "core2"] = send(piece, piece, ks.at[j, 1], kr.at[j, 1], core_peer)

    out_copies = []

    def merge(j):
        c, us, at = halves_of(j)
        rep_copies[j, "core2"].wait_recv()

        def body(k, carry):
            for u in us:
                for jc in (0, 1):
                    both = mix * loc[c, jc, k, u] + (1.0 - mix) * nxt[c, jc, k, u]
                    for e in (0, 1):
                        there = k * slab + ((2 * e + jc) * 2 + u) * SUB
                        mout[c, pl.ds(pl.multiple_of(there, SUB), SUB)] = both[e]
            return carry

        lax.fori_loop(0, nz, body, 0)
        if 1 in us:
            copy = pltpu.make_async_copy(
                mout.at[c], merged_out.at[0, :, c * cw : (c + 1) * cw], os.at[c]
            )
            copy.start()
            out_copies.append(copy)

    outer_copies = []

    def outer_send():
        for k, (src, dst) in enumerate([(anchor, anc), (outer_momentum, outer)]):
            outer_copies.append(send(src, dst.at[yl], os_.at[0, k], os_.at[1, k], lo_peer))

    def outer_wait():
        for copy in loads[4:6]:
            copy.wait()
        for copy in outer_copies:
            copy.wait_recv()

    cots_upto(1), x_upto(1), cots_upto(2)
    cot_all[:, 0:tokens] = cot_t[...]
    cots_upto(4), x_upto(4), far(0)
    x_upto(7), far(1)
    x_upto(9), near(0)
    x_upto(11), relay(0)
    near(1)
    relay(1)
    outer_send(), mine(0)
    x_upto(12), far(2)
    x_upto(13), far(3)
    near(2)
    x_upto(15), near(3)
    adam(0)
    x_upto(16), mine(1)
    relay(2)
    far(4)
    far(5)
    z_reduce(0)
    relay(3)
    near(4)
    near(5)
    mine(2)
    lo_reduce(0)
    far(6)
    relay(4)
    relay(5)
    adam(1)
    far(7)
    near(6)
    z_reduce(1)
    outer_wait(), outer_step(0)
    near(7)
    mine(3)
    relay(6)
    adam(2)
    lo_reduce(1)
    relay(7)
    z_reduce(2)
    core_gather(0)
    merge(0)
    adam(3)
    outer_step(1)
    adam(4)
    lo_reduce(2)
    z_reduce(3)
    z_reduce(4)
    outer_step(2)
    core_gather(1)
    lo_reduce(3)
    merge(1)
    outer_step(3)
    lo_reduce(4)
    outer_step(4)
    core_gather(2)
    core_gather(3)
    merge(2)
    core_gather(4)
    merge(3)
    merge(4)
    momentum_copy = pltpu.make_async_copy(momn.at[yl], momentum_out, os.at[nc])
    momentum_copy.start()
    for copy in sent:
        copy.wait_send()
    for copy in out_copies:
        copy.wait()
    momentum_copy.wait()


def per_device(features, cotangents, params, first, second, anchor, outer_momentum, step, *, nx, nz, nc):
    tokens = features.shape[0]
    rows, width = params.shape[1:]
    cw = width // nc
    piece = anchor.shape[0]
    part = rows // 2
    y_units = [(c, h * part, (h + 1) * part) for c in range(nc) for h in (0, 1)]
    r_units = [(c, (0, 1)) for c in range(nc - 1)] + [(nc - 1, (0,)), (nc - 1, (1,))]
    straight = [len(us) == 1 for c, us in r_units]
    ny_, nr_ = len(y_units), len(r_units)
    nz_ = sum(4 * nz if flag else 2 * nz for flag in straight)
    hbm = pl.BlockSpec(memory_space=pl.ANY)
    dma = pltpu.SemaphoreType.DMA
    operands = [
        pltpu.with_memory_space_constraint(a, pltpu.HBM)
        for a in (features, cotangents, params, first, second, anchor, outer_momentum)
    ]
    return pl.pallas_call(
        functools.partial(kernel, nx, nz, nc, y_units, r_units, straight),
        out_shape=(
            jax.ShapeDtypeStruct((1, rows, width), F32),
            jax.ShapeDtypeStruct((piece, width), F32),
        ),
        in_specs=[hbm] * 8,
        out_specs=(hbm, hbm),
        scratch_shapes=[
            pltpu.VMEM((tokens, rows), BF16),
            pltpu.VMEM((rows, tokens), BF16),
            pltpu.VMEM((rows, nx * tokens), BF16),
            pltpu.VMEM((NY, nx, tokens, width), BF16),
            pltpu.VMEM((rows, width), BF16),
            pltpu.VMEM((rows, width), BF16),
            pltpu.VMEM((rows, width), BF16),
            pltpu.VMEM((2, piece, width), F32),
            pltpu.VMEM((2, piece, width), F32),
            pltpu.VMEM((nc, rows, cw), F32),
            pltpu.VMEM((nc, rows, cw), F32),
            pltpu.VMEM((nc, rows, cw), BF16),
            pltpu.VMEM((nc, rows, cw), BF16),
            pltpu.VMEM((nc, rows, cw), BF16),
            pltpu.VMEM((nc, rows, cw), BF16),
            pltpu.VMEM((nc, rows, cw), BF16),
            pltpu.VMEM((nc, rows, cw), BF16),
            pltpu.VMEM((nc, 2, nz, 2, 2, SUB, cw), F32),
            pltpu.VMEM((nc, nz, 2, 2, SUB, cw), F32),
            pltpu.VMEM((nc, nz, 2, 2, SUB, cw), F32),
            pltpu.VMEM((nc, nz, 2, 2, SUB, cw), F32),
            pltpu.VMEM((nc, 2, 2, SUB, cw), F32),
            pltpu.VMEM((nc, 2, 2, SUB, cw), F32),
            pltpu.VMEM((nc, 2, nz, 2, 2, SUB, cw), F32),
            pltpu.VMEM((nc, rows, cw), F32),
            pltpu.VMEM((2, piece, width), F32),
            pltpu.SMEM((1,), jnp.int32),
            dma((7,)), dma((NY,)),
            dma((4, nx - 1)), dma((4, nx - 1)),
            dma((nc, NY, nx - 1)), dma((nc, NY, nx - 1)),
            dma((ny_, 6)), dma((ny_, 6)),
            dma((nr_, 2)), dma((nr_, 2)),
            dma((2, 2)),
            dma((nz_,)), dma((nz_,)),
            dma((nr_,)), dma((nr_,)),
            dma((nc + 1,)),
        ],
        compiler_params=pltpu.CompilerParams(
            collective_id=0, has_side_effects=True, vmem_limit_bytes=48 * 1024 * 1024
        ),
    )(*operands, step)


def build(mesh, nx, nz, nc):
    in_specs = (
        P(("replica", "fsdp"), None),
        P(("replica", "fsdp"), None),
        P("replica", None, "fsdp"),
        P("replica", None, "fsdp"),
        P("replica", None, "fsdp"),
        P("replica", "fsdp"),
        P("replica", "fsdp"),
        P(),
    )
    out_specs = (P("replica", None, "fsdp"), P("replica", "fsdp"))
    return jax.shard_map(
        functools.partial(per_device, nx=nx, nz=nz, nc=nc),
        mesh=mesh, in_specs=in_specs, out_specs=out_specs, check_vma=False,
    )


def solution(mesh):
    return build(mesh, NX, NZ, CHUNKS)
```

```python
import functools
import math

import jax
import jax.numpy as jnp
from jax import lax
from jax.experimental import pallas as pl
from jax.experimental.pallas import tpu as pltpu
from jax.sharding import PartitionSpec as P

peak_rate = 0.25
warm_steps = 8.0
beta_one = 0.9
beta_two = 0.95
decay = 0.1
outer_rate = 0.7
outer_mu = 0.9
mix = 0.5

NX, NY, NZ = 4, 4, 8
CHUNKS = 4
SUB = 8
F32, BF16 = jnp.float32, jnp.bfloat16


def kernel(
    nx, nz, nc, y_units, r_units, straight,
    feats, cots, params, first, second, anchor, outer_momentum, step,
    merged_out, momentum_out,
    cot_own, cot_t, cot_all, fbuf, par, mom1, mom2, anc, outer,
    own, keep, s1, sd, se, r1, rd, r2,
    loc, rcore, ssum, rz, tot, ry, nxt,
    step_v, in_sem, feat_sem, cs, cr, xs, xr, ys, yr, ks, kr, os_, zs, zr, ls, lr,
):
    ny = NY
    rows, width = par.shape
    cw = width // nc
    tokens = feats.shape[0]
    slab = rows // nz
    part = rows // 2
    quarter = rows // 4
    rep = lax.axis_index("replica")
    fs = lax.axis_index("fsdp")
    core = lax.rem(rep, 2)
    yl = lax.rem(lax.div(rep, 2), 2)
    z = lax.div(rep, 4)
    x = lax.div(fs, ny)
    q = lax.rem(fs, ny)

    def at_fsdp(xx, qq):
        return {"fsdp": xx * ny + qq}

    def at_rep(zz, ll, cc):
        return {"replica": zz * 4 + ll * 2 + cc}

    x_peer = [at_fsdp(lax.rem(x + d, nx), q) for d in range(nx)]
    y_up = at_fsdp(x, lax.rem(q + 1, ny))
    y_down = at_fsdp(x, lax.rem(q + ny - 1, ny))
    z_of = [lax.rem(z + d, nz) for d in range(nz)]
    z_peer = [[at_rep(zz, yl, core), at_rep(zz, 1 - yl, core)] for zz in z_of]
    core_peer = at_rep(z, yl, 1 - core)
    lo_peer = z_peer[0][1]

    loads = []
    for k, (src, dst) in enumerate(
        [
            (cots, cot_own),
            (params.at[0], par),
            (first.at[0], mom1),
            (second.at[0], mom2),
            (anchor, anc.at[yl]),
            (outer_momentum, outer.at[yl]),
            (step, step_v),
        ]
    ):
        loads.append(pltpu.make_async_copy(src, dst, in_sem.at[k]))
        loads[-1].start()

    barrier = pltpu.get_barrier_semaphore()
    peers = x_peer[1:] + [y_up, y_down, core_peer] + [p for d in range(nz) for p in z_peer[d]][1:]
    for peer in peers:
        pl.semaphore_signal(
            barrier, inc=1, device_id=peer, device_id_type=pl.DeviceIdType.MESH
        )

    def owner_cols(xx, o):
        return pl.multiple_of((xx * ny + lax.rem(q + o, ny)) * width, width)

    own_feats = []
    for o in range(ny):
        own_feats.append(
            pltpu.make_async_copy(
                feats.at[:, pl.ds(owner_cols(x, o), width)],
                fbuf.at[o, 0],
                feat_sem.at[o],
            )
        )
        own_feats[-1].start()

    sent = []

    def send(src, dst, ssem, rsem, peer):
        copy = pltpu.make_async_remote_copy(
            src_ref=src,
            dst_ref=dst,
            send_sem=ssem,
            recv_sem=rsem,
            device_id=peer,
            device_id_type=pl.DeviceIdType.MESH,
        )
        copy.start()
        sent.append(copy)
        return copy

    loads[0].wait()
    turned = cot_own[...].astype(F32).T.reshape(4 * nz, 2, SUB, tokens)
    for u in (0, 1):
        cot_t[u * part : (u + 1) * part] = turned[:, u].reshape(part, tokens).astype(BF16)

    pl.semaphore_wait(barrier, len(peers))

    cot_copies = {}

    def cot_send(k):
        some = slice(k * quarter, (k + 1) * quarter)
        cot_copies[k] = [
            send(
                cot_t.at[some],
                cot_all.at[some, d * tokens : (d + 1) * tokens],
                cs.at[k, d - 1],
                cr.at[k, d - 1],
                x_peer[d],
            )
            for d in range(1, nx)
        ]

    x_copies = {}

    def x_send(c, o):
        x_copies[c, o] = [
            send(
                feats.at[:, pl.ds(owner_cols(lax.rem(x + d, nx), o) + c * cw, cw)],
                fbuf.at[o, d, :, c * cw : (c + 1) * cw],
                xs.at[c, o, d - 1],
                xr.at[c, o, d - 1],
                x_peer[d],
            )
            for d in range(1, nx)
        ]

    x_order = []
    for i, (c, lo, hi) in enumerate(y_units):
        ahead = y_units[: i + 2]
        uses = [(a[0], 2) for a in ahead] + [(c, o) for o in (1, 3, 0)]
        for use in uses:
            if use not in x_order:
                x_order.append(use)
    x_done, cots_done = [0], [0]

    def x_upto(n):
        for use in x_order[x_done[0] : n]:
            x_send(*use)
        x_done[0] = max(x_done[0], n)

    def cots_upto(n):
        for k in range(cots_done[0], n):
            cot_send(k)
        cots_done[0] = max(cots_done[0], n)

    arrived = set()

    def block(c, o):
        x_upto(x_order.index((c, o)) + 1)
        if (c, o) not in arrived:
            arrived.add((c, o))
            if c == 0:
                own_feats[o].wait()
            for copy in x_copies[c, o]:
                copy.wait_recv()
        return fbuf[o, :, :, c * cw : (c + 1) * cw].reshape(nx * tokens, cw)

    def dot(lo, hi, cols):
        for k in range(lo // quarter, -(-hi // quarter)):
            for copy in cot_copies.pop(k, []):
                copy.wait_recv()
        return jnp.dot(cot_all[lo:hi], cols, preferred_element_type=F32)

    y_copies = {}

    def y_halves(i):
        c, lo, hi = y_units[i]
        mid = (lo + hi) // 2
        return c, (lo, mid), (mid, hi)

    def y_send(i, k, c, some, src, dst, peer):
        here = slice(*some)
        y_copies[i, k] = send(
            src.at[c, here], dst.at[c, here], ys.at[i, k], yr.at[i, k], peer
        )

    def far(i):
        c, a, b = y_halves(i)
        cols = block(c, 2)
        for k, some, peer in ((0, a, y_down), (1, b, y_up)):
            s1[c, slice(*some)] = dot(*some, cols).astype(BF16)
            y_send(i, k, c, some, s1, r1, peer)

    def near(i):
        c, a, b = y_halves(i)
        for k, o, direct, kept, peer in ((2, 1, a, b, y_up), (3, 3, b, a, y_down)):
            cols = block(c, o)
            sd[c, slice(*direct)] = dot(*direct, cols).astype(BF16)
            y_send(i, k, c, direct, sd, rd, peer)
            keep[c, slice(*kept)] = dot(*kept, cols)

    def relay(i):
        c, a, b = y_halves(i)
        for k, some, peer in ((0, a, y_down), (1, b, y_up)):
            here = slice(*some)
            y_copies[i, k].wait_recv()
            se[c, here] = (keep[c, here] + r1[c, here].astype(F32)).astype(BF16)
            y_send(i, 4 + k, c, some, se, r2, peer)

    def mine(c):
        cols = block(c, 0)
        for h in (0, 1):
            own[c, h * part : (h + 1) * part] = dot(h * part, (h + 1) * part, cols)

    rep_copies = {}

    def halves_of(j):
        c, us = r_units[j]
        return c, us, (slice(None) if len(us) == 2 else us[0])

    def adam(j):
        c, us, at = halves_of(j)
        if j == 0:
            for k in (1, 2, 3, 6):
                loads[k].wait()
        for i, (cc, lo, hi) in enumerate(y_units):
            if cc == c and any(lo < (u + 1) * part and u * part < hi for u in us):
                for k in (2, 3, 4, 5):
                    y_copies[i, k].wait_recv()
        t_value = jnp.full((1, cw), step_v[0].astype(F32), F32)
        rate = peak_rate * jnp.minimum(1.0, t_value / warm_steps)
        inv_one = 1.0 / (1.0 - jnp.exp(t_value * math.log(beta_one)))
        inv_two = 1.0 / (1.0 - jnp.exp(t_value * math.log(beta_two)))
        cols = slice(c * cw, (c + 1) * cw)

        def body(k, carry):
            here = pl.ds(pl.multiple_of(k * slab, slab), slab)
            for u in us:
                def rows_of(ref):
                    strip = ref[here, cols].astype(F32).reshape(4, 2, SUB, cw)
                    return strip[:, u].reshape(4 * SUB, cw)

                there = pl.ds(pl.multiple_of(u * part + k * (slab // 2), slab // 2), slab // 2)
                grad = own[c, there] + rd[c, there].astype(F32) + r2[c, there].astype(F32)
                weight = rows_of(par)
                m = beta_one * rows_of(mom1) + (1.0 - beta_one) * grad
                v = beta_two * rows_of(mom2) + (1.0 - beta_two) * grad * grad
                update = (m * inv_one) / (jnp.sqrt(v * inv_two) + 1e-08)
                new = weight - rate * (update + decay * weight)
                new = new.reshape(2, 2, SUB, cw)
                loc[c, 0, k, u] = new[:, 0]
                loc[c, 1, k, u] = new[:, 1]
            return carry

        lax.fori_loop(0, nz, body, 0)
        rep_copies[j, "core"] = send(
            loc.at[c, 1 - core, :, at], rcore.at[c, :, at], ks.at[j, 0], kr.at[j, 0], core_peer
        )

    z_first = [0]
    for flag in straight:
        z_first.append(z_first[-1] + (4 if flag else 2) * nz)

    def z_send(j, stage, d, e, src, dst):
        at = z_first[j] + ((stage * nz + d) * 2 + e if straight[j] else stage * nz + d)
        return send(src, dst, zs.at[at], zr.at[at], z_peer[d][e])

    def z_reduce(j):
        c, us, at = halves_of(j)
        rep_copies[j, "core"].wait_recv()
        copies = []
        for d in sorted(range(nz), key=lambda d: -min(d, nz - d)):
            zz = z_of[d]
            ssum[c, zz, at] = loc[c, core, zz, at] + rcore[c, zz, at]
            for e in (0, 1) if straight[j] else (0,):
                if d or e:
                    lo = (1 - yl if e else yl) if straight[j] else slice(None)
                    to = e if straight[j] else slice(None)
                    copies.append(
                        z_send(j, 0, d, e, ssum.at[c, zz, at, lo], rz.at[c, d, at, to])
                    )
        rep_copies[j, "z"] = copies

    def lo_reduce(j):
        c, us, at = halves_of(j)
        for copy in rep_copies[j, "z"]:
            copy.wait_recv()
        if straight[j]:
            total = ssum[c, z, at, yl] + rz[c, 0, at, 1]
            for d in range(1, nz):
                total = total + (rz[c, d, at, 0] + rz[c, d, at, 1])
            tot[c, at, 0] = total
        else:
            total = ssum[c, z, at]
            for d in range(1, nz):
                total = total + rz[c, d, at]
            tot[c, at] = total
            rep_copies[j, "lo"] = send(tot.at[c, at], ry.at[c, at], ls.at[j], lr.at[j], lo_peer)

    def outer_step(j):
        c, us, at = halves_of(j)
        cols = slice(c * cw, (c + 1) * cw)
        if not straight[j]:
            rep_copies[j, "lo"].wait_recv()
        for u in us:
            some = slice(u * SUB, (u + 1) * SUB)
            if straight[j]:
                total, who = tot[c, u, 0], yl
            else:
                total, who = tot[c, u] + ry[c, u], slice(None)
            old = anc[who, some, cols]
            delta = old - total * (1.0 / (4 * nz))
            momentum = outer_mu * outer[who, some, cols] + delta
            nxt[c, core, z, u, who] = old - outer_rate * (delta + outer_mu * momentum)
            momentum_out[some, cols] = momentum if straight[j] else jnp.where(yl == 0, momentum[0], momentum[1])
        piece = nxt.at[c, core, z, at, yl] if straight[j] else nxt.at[c, core, z, at]
        rep_copies[j, "z2"] = [
            z_send(j, 1, d, e, piece, piece)
            for d in sorted(range(nz), key=lambda d: -min(d, nz - d))
            for e in ((0, 1) if straight[j] else (0,))
            if d or e
        ]

    def core_gather(j):
        c, us, at = halves_of(j)
        for copy in rep_copies[j, "z2"]:
            copy.wait_recv()
        piece = nxt.at[c, core, :, at]
        rep_copies[j, "core2"] = send(piece, piece, ks.at[j, 1], kr.at[j, 1], core_peer)

    def merge(j):
        c, us, at = halves_of(j)
        rep_copies[j, "core2"].wait_recv()
        cols = slice(c * cw, (c + 1) * cw)

        def body(k, carry):
            for u in us:
                for jc in (0, 1):
                    both = mix * loc[c, jc, k, u] + (1.0 - mix) * nxt[c, jc, k, u]
                    for e in (0, 1):
                        there = k * slab + ((2 * e + jc) * 2 + u) * SUB
                        merged_out[0, pl.ds(pl.multiple_of(there, SUB), SUB), cols] = both[e]
            return carry

        lax.fori_loop(0, nz, body, 0)

    outer_copies = []

    def outer_send():
        for k, (src, dst) in enumerate([(anchor, anc), (outer_momentum, outer)]):
            outer_copies.append(send(src, dst.at[yl], os_.at[0, k], os_.at[1, k], lo_peer))

    def outer_wait():
        for copy in loads[4:6]:
            copy.wait()
        for copy in outer_copies:
            copy.wait_recv()

    cots_upto(1), x_upto(1), cots_upto(2)
    cot_all[:, 0:tokens] = cot_t[...]
    x_upto(3), far(0)
    cots_upto(4), x_upto(4), near(0)
    x_upto(6), relay(0)
    far(1)
    x_upto(8), near(1)
    outer_send(), mine(0)
    x_upto(9), far(2)
    x_upto(10), relay(1)
    far(3)
    x_upto(11), near(2)
    x_upto(13), mine(1)
    x_upto(14), adam(0)
    relay(2)
    x_upto(15), z_reduce(0)
    far(4)
    x_upto(16), near(3)
    mine(2)
    lo_reduce(0)
    adam(1)
    relay(3)
    z_reduce(1)
    far(5)
    outer_wait(), outer_step(0)
    near(4)
    relay(4)
    adam(2)
    lo_reduce(1)
    near(5)
    mine(3)
    z_reduce(2)
    relay(5)
    core_gather(0)
    adam(3)
    outer_step(1)
    merge(0)
    z_reduce(3)
    adam(4)
    lo_reduce(2)
    z_reduce(4)
    outer_step(2)
    core_gather(1)
    lo_reduce(3)
    outer_step(3)
    merge(1)
    lo_reduce(4)
    outer_step(4)
    core_gather(2)
    core_gather(3)
    merge(2)
    core_gather(4)
    merge(3)
    merge(4)
    for copy in sent:
        copy.wait_send()


def per_device(features, cotangents, params, first, second, anchor, outer_momentum, step, *, nx, nz, nc):
    tokens = features.shape[0]
    rows, width = params.shape[1:]
    cw = width // nc
    piece = anchor.shape[0]
    part = rows // 2
    y_units = [(0, 0, part), (0, part, rows)]
    y_units += [(c, 0, rows) for c in range(1, nc - 1)]
    y_units += [(nc - 1, 0, part), (nc - 1, part, rows)]
    r_units = [(c, (0, 1)) for c in range(nc - 1)] + [(nc - 1, (0,)), (nc - 1, (1,))]
    straight = [len(us) == 1 for c, us in r_units]
    ny_, nr_ = len(y_units), len(r_units)
    nz_ = sum(4 * nz if flag else 2 * nz for flag in straight)
    hbm = pl.BlockSpec(memory_space=pl.ANY)
    dma = pltpu.SemaphoreType.DMA
    operands = [
        pltpu.with_memory_space_constraint(a, pltpu.HBM)
        for a in (features, cotangents, params, first, second, anchor, outer_momentum)
    ]
    return pl.pallas_call(
        functools.partial(kernel, nx, nz, nc, y_units, r_units, straight),
        out_shape=(
            jax.ShapeDtypeStruct((1, rows, width), F32),
            jax.ShapeDtypeStruct((piece, width), F32),
        ),
        in_specs=[hbm] * 8,
        out_specs=(pl.BlockSpec(memory_space=pltpu.VMEM),) * 2,
        scratch_shapes=[
            pltpu.VMEM((tokens, rows), BF16),
            pltpu.VMEM((rows, tokens), BF16),
            pltpu.VMEM((rows, nx * tokens), BF16),
            pltpu.VMEM((NY, nx, tokens, width), BF16),
            pltpu.VMEM((rows, width), BF16),
            pltpu.VMEM((rows, width), BF16),
            pltpu.VMEM((rows, width), BF16),
            pltpu.VMEM((2, piece, width), F32),
            pltpu.VMEM((2, piece, width), F32),
            pltpu.VMEM((nc, rows, cw), F32),
            pltpu.VMEM((nc, rows, cw), F32),
            pltpu.VMEM((nc, rows, cw), BF16),
            pltpu.VMEM((nc, rows, cw), BF16),
            pltpu.VMEM((nc, rows, cw), BF16),
            pltpu.VMEM((nc, rows, cw), BF16),
            pltpu.VMEM((nc, rows, cw), BF16),
            pltpu.VMEM((nc, rows, cw), BF16),
            pltpu.VMEM((nc, 2, nz, 2, 2, SUB, cw), F32),
            pltpu.VMEM((nc, nz, 2, 2, SUB, cw), F32),
            pltpu.VMEM((nc, nz, 2, 2, SUB, cw), F32),
            pltpu.VMEM((nc, nz, 2, 2, SUB, cw), F32),
            pltpu.VMEM((nc, 2, 2, SUB, cw), F32),
            pltpu.VMEM((nc, 2, 2, SUB, cw), F32),
            pltpu.VMEM((nc, 2, nz, 2, 2, SUB, cw), F32),
            pltpu.SMEM((1,), jnp.int32),
            dma((7,)), dma((NY,)),
            dma((4, nx - 1)), dma((4, nx - 1)),
            dma((nc, NY, nx - 1)), dma((nc, NY, nx - 1)),
            dma((ny_, 6)), dma((ny_, 6)),
            dma((nr_, 2)), dma((nr_, 2)),
            dma((2, 2)),
            dma((nz_,)), dma((nz_,)),
            dma((nr_,)), dma((nr_,)),
        ],
        compiler_params=pltpu.CompilerParams(
            collective_id=0, has_side_effects=True, vmem_limit_bytes=48 * 1024 * 1024
        ),
    )(*operands, step)


def build(mesh, nx, nz, nc):
    in_specs = (
        P(("replica", "fsdp"), None),
        P(("replica", "fsdp"), None),
        P("replica", None, "fsdp"),
        P("replica", None, "fsdp"),
        P("replica", None, "fsdp"),
        P("replica", "fsdp"),
        P("replica", "fsdp"),
        P(),
    )
    out_specs = (P("replica", None, "fsdp"), P("replica", "fsdp"))
    return jax.shard_map(
        functools.partial(per_device, nx=nx, nz=nz, nc=nc),
        mesh=mesh, in_specs=in_specs, out_specs=out_specs, check_vma=False,
    )


def solution(mesh):
    return build(mesh, NX, NZ, CHUNKS)
```

```python
import functools
import math

import jax
import jax.numpy as jnp
from jax import lax
from jax.experimental import pallas as pl
from jax.experimental.pallas import tpu as pltpu
from jax.sharding import PartitionSpec as P

peak_rate = 0.25
warm_steps = 8.0
beta_one = 0.9
beta_two = 0.95
decay = 0.1
outer_rate = 0.7
outer_mu = 0.9
mix = 0.5

NX, NY, NZ = 4, 4, 8
CHUNKS = 4
SUB = 8
F32, BF16 = jnp.float32, jnp.bfloat16


def kernel(
    nx, nz, nc, y_units, r_units, straight, split,
    feats, cots, params, first, second, anchor, outer_momentum, step,
    merged_out, momentum_out,
    cot_own, cot_t, cot_all, fbuf, par, mom1, mom2, anc, outer,
    own, keep, s1, sd, se, r1, rd, r2,
    loc, rcore, ssum, rz, tot, ry, nxt,
    step_v, in_sem, feat_sem, cs, cr, xs, xr, ys, yr, ks, kr, os_, zs, zr, ls, lr,
):
    ny = NY
    rows, width = par.shape
    cw = width // nc
    tokens = feats.shape[0]
    slab = rows // nz
    part = rows // 2
    quarter = rows // 4
    rep = lax.axis_index("replica")
    fs = lax.axis_index("fsdp")
    core = lax.rem(rep, 2)
    yl = lax.rem(lax.div(rep, 2), 2)
    z = lax.div(rep, 4)
    x = lax.div(fs, ny)
    q = lax.rem(fs, ny)

    def at_fsdp(xx, qq):
        return {"fsdp": xx * ny + qq}

    def at_rep(zz, ll, cc):
        return {"replica": zz * 4 + ll * 2 + cc}

    x_peer = [at_fsdp(lax.rem(x + d, nx), q) for d in range(nx)]
    y_up = at_fsdp(x, lax.rem(q + 1, ny))
    y_down = at_fsdp(x, lax.rem(q + ny - 1, ny))
    z_of = [lax.rem(z + d, nz) for d in range(nz)]
    z_peer = [[at_rep(zz, yl, core), at_rep(zz, 1 - yl, core)] for zz in z_of]
    core_peer = at_rep(z, yl, 1 - core)
    lo_peer = z_peer[0][1]

    loads = []
    for k, (src, dst) in enumerate(
        [
            (cots, cot_own),
            (params.at[0], par),
            (first.at[0], mom1),
            (second.at[0], mom2),
            (anchor, anc.at[yl]),
            (outer_momentum, outer.at[yl]),
            (step, step_v),
        ]
    ):
        loads.append(pltpu.make_async_copy(src, dst, in_sem.at[k]))
        if k == 0:
            loads[-1].start()

    barrier = pltpu.get_barrier_semaphore()
    peers = x_peer[1:] + [y_up, y_down, core_peer] + [p for d in range(nz) for p in z_peer[d]][1:]
    for peer in peers:
        pl.semaphore_signal(
            barrier, inc=1, device_id=peer, device_id_type=pl.DeviceIdType.MESH
        )

    def owner_cols(xx, o):
        return pl.multiple_of((xx * ny + lax.rem(q + o, ny)) * width, width)

    own_feats = []
    for o in range(ny):
        own_feats.append(
            pltpu.make_async_copy(
                feats.at[:, pl.ds(owner_cols(x, o), width)],
                fbuf.at[o, 0],
                feat_sem.at[o],
            )
        )
        own_feats[-1].start()

    sent = []

    def send(src, dst, ssem, rsem, peer):
        copy = pltpu.make_async_remote_copy(
            src_ref=src,
            dst_ref=dst,
            send_sem=ssem,
            recv_sem=rsem,
            device_id=peer,
            device_id_type=pl.DeviceIdType.MESH,
        )
        copy.start()
        sent.append(copy)
        return copy

    loads[0].wait()
    turned = cot_own[...].astype(F32).T.reshape(4 * nz, 2, SUB, tokens)
    for u in (0, 1):
        cot_t[u * part : (u + 1) * part] = turned[:, u].reshape(part, tokens).astype(BF16)

    pl.semaphore_wait(barrier, len(peers))

    cot_copies = {}

    def cot_send(k):
        some = slice(k * quarter, (k + 1) * quarter)
        cot_copies[k] = [
            send(
                cot_t.at[some],
                cot_all.at[some, d * tokens : (d + 1) * tokens],
                cs.at[k, d - 1],
                cr.at[k, d - 1],
                x_peer[d],
            )
            for d in range(1, nx)
        ]

    x_copies = {}

    def x_send(c, o):
        x_copies[c, o] = [
            send(
                feats.at[:, pl.ds(owner_cols(lax.rem(x + d, nx), o) + c * cw, cw)],
                fbuf.at[o, d, :, c * cw : (c + 1) * cw],
                xs.at[c, o, d - 1],
                xr.at[c, o, d - 1],
                x_peer[d],
            )
            for d in range(1, nx)
        ]

    x_order = []
    for i, (c, lo, hi) in enumerate(y_units):
        ahead = y_units[: i + 2]
        uses = [(a[0], 2) for a in ahead] + [(c, o) for o in (1, 3, 0)]
        for use in uses:
            if use not in x_order:
                x_order.append(use)
    x_done, cots_done = [0], [0]

    def x_upto(n):
        for use in x_order[x_done[0] : n]:
            x_send(*use)
        x_done[0] = max(x_done[0], n)

    def cots_upto(n):
        for k in range(cots_done[0], n):
            cot_send(k)
        cots_done[0] = max(cots_done[0], n)

    arrived = set()

    def block(c, o):
        x_upto(x_order.index((c, o)) + 1)
        if (c, o) not in arrived:
            arrived.add((c, o))
            if c == 0:
                own_feats[o].wait()
            for copy in x_copies[c, o]:
                copy.wait_recv()
        return fbuf[o, :, :, c * cw : (c + 1) * cw].reshape(nx * tokens, cw)

    def dot(lo, hi, cols):
        for k in range(lo // quarter, -(-hi // quarter)):
            for copy in cot_copies.pop(k, []):
                copy.wait_recv()
        return jnp.dot(cot_all[lo:hi], cols, preferred_element_type=F32)

    y_copies = {}

    def y_halves(i):
        c, lo, hi = y_units[i]
        mid = (lo + hi) // 2
        return c, (lo, mid), (mid, hi)

    def y_send(i, k, c, some, src, dst, peer):
        here = slice(*some)
        y_copies[i, k] = send(
            src.at[c, here], dst.at[c, here], ys.at[i, k], yr.at[i, k], peer
        )

    def far(i):
        c, a, b = y_halves(i)
        cols = block(c, 2)
        for k, some, peer in ((0, a, y_down), (1, b, y_up)):
            s1[c, slice(*some)] = dot(*some, cols).astype(BF16)
            y_send(i, k, c, some, s1, r1, peer)

    def near(i):
        c, a, b = y_halves(i)
        for k, o, direct, kept, peer in ((2, 1, a, b, y_up), (3, 3, b, a, y_down)):
            cols = block(c, o)
            sd[c, slice(*direct)] = dot(*direct, cols).astype(BF16)
            y_send(i, k, c, direct, sd, rd, peer)
            keep[c, slice(*kept)] = dot(*kept, cols)

    def relay(i):
        c, a, b = y_halves(i)
        for k, some, peer in ((0, a, y_down), (1, b, y_up)):
            here = slice(*some)
            y_copies[i, k].wait_recv()
            se[c, here] = (keep[c, here] + r1[c, here].astype(F32)).astype(BF16)
            y_send(i, 4 + k, c, some, se, r2, peer)

    def mine(c):
        cols = block(c, 0)
        for h in (0, 1):
            own[c, h * part : (h + 1) * part] = dot(h * part, (h + 1) * part, cols)

    rep_copies = {}

    def halves_of(j):
        c, us = r_units[j]
        return c, us, (slice(None) if len(us) == 2 else us[0])

    def adam(j):
        c, us, at = halves_of(j)
        if j == 0:
            for k in (1, 2, 3, 6):
                loads[k].wait()
        for i, (cc, lo, hi) in enumerate(y_units):
            if cc == c and any(lo < (u + 1) * part and u * part < hi for u in us):
                for k in (2, 3, 4, 5):
                    y_copies[i, k].wait_recv()
        t_value = jnp.full((1, cw), step_v[0].astype(F32), F32)
        rate = peak_rate * jnp.minimum(1.0, t_value / warm_steps)
        inv_one = 1.0 / (1.0 - jnp.exp(t_value * math.log(beta_one)))
        inv_two = 1.0 / (1.0 - jnp.exp(t_value * math.log(beta_two)))
        cols = slice(c * cw, (c + 1) * cw)

        def body(k, carry):
            here = pl.ds(pl.multiple_of(k * slab, slab), slab)
            for u in us:
                def rows_of(ref):
                    strip = ref[here, cols].astype(F32).reshape(4, 2, SUB, cw)
                    return strip[:, u].reshape(4 * SUB, cw)

                there = pl.ds(pl.multiple_of(u * part + k * (slab // 2), slab // 2), slab // 2)
                grad = own[c, there] + rd[c, there].astype(F32) + r2[c, there].astype(F32)
                weight = rows_of(par)
                m = beta_one * rows_of(mom1) + (1.0 - beta_one) * grad
                v = beta_two * rows_of(mom2) + (1.0 - beta_two) * grad * grad
                update = (m * inv_one) / (jnp.sqrt(v * inv_two) + 1e-08)
                new = weight - rate * (update + decay * weight)
                new = new.reshape(2, 2, SUB, cw)
                loc[c, 0, k, u] = new[:, 0]
                loc[c, 1, k, u] = new[:, 1]
            return carry

        lax.fori_loop(0, nz, body, 0)
        rep_copies[j, "core"] = send(
            loc.at[c, 1 - core, :, at], rcore.at[c, :, at], ks.at[j, 0], kr.at[j, 0], core_peer
        )

    z_first = [0]
    for flag in straight:
        z_first.append(z_first[-1] + (4 if flag else 2) * nz)

    def z_send(j, stage, d, e, src, dst):
        at = z_first[j] + ((stage * nz + d) * 2 + e if straight[j] else stage * nz + d)
        return send(src, dst, zs.at[at], zr.at[at], z_peer[d][e])

    def z_reduce(j):
        c, us, at = halves_of(j)
        rep_copies[j, "core"].wait_recv()
        copies = []
        for d in sorted(range(nz), key=lambda d: -min(d, nz - d)):
            zz = z_of[d]
            ssum[c, zz, at] = loc[c, core, zz, at] + rcore[c, zz, at]
            for e in (0, 1) if straight[j] else (0,):
                if d or e:
                    lo = (1 - yl if e else yl) if straight[j] else slice(None)
                    to = e if straight[j] else slice(None)
                    copies.append(
                        z_send(j, 0, d, e, ssum.at[c, zz, at, lo], rz.at[c, d, at, to])
                    )
        rep_copies[j, "z"] = copies

    def lo_reduce(j):
        c, us, at = halves_of(j)
        for copy in rep_copies[j, "z"]:
            copy.wait_recv()
        if straight[j]:
            total = ssum[c, z, at, yl] + rz[c, 0, at, 1]
            for d in range(1, nz):
                total = total + (rz[c, d, at, 0] + rz[c, d, at, 1])
            tot[c, at, 0] = total
        else:
            total = ssum[c, z, at]
            for d in range(1, nz):
                total = total + rz[c, d, at]
            tot[c, at] = total
            rep_copies[j, "lo"] = send(tot.at[c, at], ry.at[c, at], ls.at[0, j], lr.at[0, j], lo_peer)

    def outer_step(j):
        c, us, at = halves_of(j)
        cols = slice(c * cw, (c + 1) * cw)
        if not straight[j]:
            rep_copies[j, "lo"].wait_recv()
        for u in us:
            some = slice(u * SUB, (u + 1) * SUB)
            if straight[j]:
                total, who = tot[c, u, 0], yl
            elif split[j]:
                total, who = tot[c, u, yl] + ry[c, u, yl], yl
            else:
                total, who = tot[c, u] + ry[c, u], slice(None)
            old = anc[who, some, cols]
            delta = old - total * (1.0 / (4 * nz))
            momentum = outer_mu * outer[who, some, cols] + delta
            nxt[c, core, z, u, who] = old - outer_rate * (delta + outer_mu * momentum)
            momentum_out[some, cols] = momentum if straight[j] or split[j] else jnp.where(yl == 0, momentum[0], momentum[1])
        piece = nxt.at[c, core, z, at, yl] if straight[j] or split[j] else nxt.at[c, core, z, at]
        rep_copies[j, "z2"] = [
            z_send(j, 1, d, e, piece, piece)
            for d in sorted(range(nz), key=lambda d: -min(d, nz - d))
            for e in ((0, 1) if straight[j] else (0,))
            if d or e
        ]

    def lo_gather(j):
        c, us, at = halves_of(j)
        for copy in rep_copies[j, "z2"]:
            copy.wait_recv()
        piece = nxt.at[c, core, :, at, yl]
        rep_copies[j, "lo2"] = send(piece, piece, ls.at[1, j], lr.at[1, j], lo_peer)

    def core_gather(j):
        c, us, at = halves_of(j)
        for copy in [rep_copies[j, "lo2"]] if split[j] else rep_copies[j, "z2"]:
            copy.wait_recv()
        piece = nxt.at[c, core, :, at]
        rep_copies[j, "core2"] = send(piece, piece, ks.at[j, 1], kr.at[j, 1], core_peer)

    def merge(j):
        c, us, at = halves_of(j)
        rep_copies[j, "core2"].wait_recv()
        cols = slice(c * cw, (c + 1) * cw)

        def body(k, carry):
            for u in us:
                for jc in (0, 1):
                    both = mix * loc[c, jc, k, u] + (1.0 - mix) * nxt[c, jc, k, u]
                    for e in (0, 1):
                        there = k * slab + ((2 * e + jc) * 2 + u) * SUB
                        merged_out[0, pl.ds(pl.multiple_of(there, SUB), SUB), cols] = both[e]
            return carry

        lax.fori_loop(0, nz, body, 0)

    outer_copies = []

    def outer_send():
        for k, (src, dst) in enumerate([(anchor, anc), (outer_momentum, outer)]):
            outer_copies.append(send(src, dst.at[yl], os_.at[0, k], os_.at[1, k], lo_peer))

    def outer_wait():
        for copy in loads[4:6]:
            copy.wait()
        for copy in outer_copies:
            copy.wait_recv()

    cots_upto(1), x_upto(1), cots_upto(2)
    cot_all[:, 0:tokens] = cot_t[...]
    x_upto(3), far(0)
    for copy in loads[1:]:
        copy.start()
    cots_upto(4), x_upto(4), near(0)
    x_upto(6), relay(0)
    far(1)
    x_upto(8), near(1)
    outer_send(), mine(0)
    x_upto(9), far(2)
    x_upto(10), relay(1)
    far(3)
    x_upto(11), near(2)
    x_upto(13), mine(1)
    x_upto(14), adam(0)
    relay(2)
    x_upto(15), z_reduce(0)
    far(4)
    x_upto(16), near(3)
    mine(2)
    lo_reduce(0)
    adam(1)
    relay(3)
    z_reduce(1)
    far(5)
    outer_wait(), outer_step(0)
    near(4)
    relay(4)
    adam(2)
    lo_reduce(1)
    z_reduce(2)
    near(5)
    mine(3)
    relay(5)
    core_gather(0)
    adam(3)
    outer_step(1)
    merge(0)
    z_reduce(3)
    adam(4)
    lo_reduce(2)
    z_reduce(4)
    outer_step(2)
    lo_gather(1)
    lo_reduce(3)
    outer_step(3)
    core_gather(1)
    lo_reduce(4)
    outer_step(4)
    lo_gather(2)
    merge(1)
    core_gather(3)
    core_gather(2)
    core_gather(4)
    merge(3)
    merge(2)
    merge(4)
    for copy in sent:
        copy.wait_send()


def per_device(features, cotangents, params, first, second, anchor, outer_momentum, step, *, nx, nz, nc):
    tokens = features.shape[0]
    rows, width = params.shape[1:]
    cw = width // nc
    piece = anchor.shape[0]
    part = rows // 2
    y_units = [(0, 0, part), (0, part, rows)]
    y_units += [(c, 0, rows) for c in range(1, nc - 1)]
    y_units += [(nc - 1, 0, part), (nc - 1, part, rows)]
    r_units = [(c, (0, 1)) for c in range(nc - 1)] + [(nc - 1, (0,)), (nc - 1, (1,))]
    straight = [len(us) == 1 for c, us in r_units]
    split = [0 < c < nc - 1 for c, us in r_units]
    ny_, nr_ = len(y_units), len(r_units)
    nz_ = sum(4 * nz if flag else 2 * nz for flag in straight)
    hbm = pl.BlockSpec(memory_space=pl.ANY)
    dma = pltpu.SemaphoreType.DMA
    operands = [
        pltpu.with_memory_space_constraint(a, pltpu.HBM)
        for a in (features, cotangents, params, first, second, anchor, outer_momentum)
    ]
    return pl.pallas_call(
        functools.partial(kernel, nx, nz, nc, y_units, r_units, straight, split),
        out_shape=(
            jax.ShapeDtypeStruct((1, rows, width), F32),
            jax.ShapeDtypeStruct((piece, width), F32),
        ),
        in_specs=[hbm] * 8,
        out_specs=(pl.BlockSpec(memory_space=pltpu.VMEM),) * 2,
        scratch_shapes=[
            pltpu.VMEM((tokens, rows), BF16),
            pltpu.VMEM((rows, tokens), BF16),
            pltpu.VMEM((rows, nx * tokens), BF16),
            pltpu.VMEM((NY, nx, tokens, width), BF16),
            pltpu.VMEM((rows, width), BF16),
            pltpu.VMEM((rows, width), BF16),
            pltpu.VMEM((rows, width), BF16),
            pltpu.VMEM((2, piece, width), F32),
            pltpu.VMEM((2, piece, width), F32),
            pltpu.VMEM((nc, rows, cw), F32),
            pltpu.VMEM((nc, rows, cw), F32),
            pltpu.VMEM((nc, rows, cw), BF16),
            pltpu.VMEM((nc, rows, cw), BF16),
            pltpu.VMEM((nc, rows, cw), BF16),
            pltpu.VMEM((nc, rows, cw), BF16),
            pltpu.VMEM((nc, rows, cw), BF16),
            pltpu.VMEM((nc, rows, cw), BF16),
            pltpu.VMEM((nc, 2, nz, 2, 2, SUB, cw), F32),
            pltpu.VMEM((nc, nz, 2, 2, SUB, cw), F32),
            pltpu.VMEM((nc, nz, 2, 2, SUB, cw), F32),
            pltpu.VMEM((nc, nz, 2, 2, SUB, cw), F32),
            pltpu.VMEM((nc, 2, 2, SUB, cw), F32),
            pltpu.VMEM((nc, 2, 2, SUB, cw), F32),
            pltpu.VMEM((nc, 2, nz, 2, 2, SUB, cw), F32),
            pltpu.SMEM((1,), jnp.int32),
            dma((7,)), dma((NY,)),
            dma((4, nx - 1)), dma((4, nx - 1)),
            dma((nc, NY, nx - 1)), dma((nc, NY, nx - 1)),
            dma((ny_, 6)), dma((ny_, 6)),
            dma((nr_, 2)), dma((nr_, 2)),
            dma((2, 2)),
            dma((nz_,)), dma((nz_,)),
            dma((2, nr_)), dma((2, nr_)),
        ],
        compiler_params=pltpu.CompilerParams(
            collective_id=0, has_side_effects=True, vmem_limit_bytes=48 * 1024 * 1024
        ),
    )(*operands, step)


def build(mesh, nx, nz, nc):
    in_specs = (
        P(("replica", "fsdp"), None),
        P(("replica", "fsdp"), None),
        P("replica", None, "fsdp"),
        P("replica", None, "fsdp"),
        P("replica", None, "fsdp"),
        P("replica", "fsdp"),
        P("replica", "fsdp"),
        P(),
    )
    out_specs = (P("replica", None, "fsdp"), P("replica", "fsdp"))
    return jax.shard_map(
        functools.partial(per_device, nx=nx, nz=nz, nc=nc),
        mesh=mesh, in_specs=in_specs, out_specs=out_specs, check_vma=False,
    )


def solution(mesh):
    return build(mesh, NX, NZ, CHUNKS)
```
